512 devices in a mesh: ctx: 64 (over y, x, core), head: 8 (over z).
Axes of the slice: x: 4, y: 8, z: 8, core: 2. Of those that a mesh axis runs over, the one named last changes fastest.
Arguments:
- queries: bfloat16 [8192, 8192], P('ctx', 'head'), may hold values from -21 to 21
- key_cache: bfloat16 [32768, 1024], P('ctx', 'head'), may hold values from -21 to 21
- value_cache: bfloat16 [32768, 1024], P('ctx', 'head'), may hold values from -18 to 18
- offsets: int32 [1024], P('ctx'), may hold values from 0 to 504
- selected: int32 [1024, 8], P('ctx'), may hold values from -1 to 63, as said below
- out_gain: bfloat16 [8192], P('head'), may hold values from 0.5 to 1.5
Outputs:
- normed_out: bfloat16 [8192, 8192], P('ctx', 'head')
The draws below stay inside these ranges and needn't reach their ends.
Inputs may be any that keep to these rules, and one draw needn't show every extreme that they name: Entry 0 of row g is the query block's own key block g // 16; the other entries are distinct key blocks below it, followed by -1 for unused entries. Among the query blocks of one index of ctx, at most 2 select any one key block in entries 1 and later, and some device has a block selected exactly 2 times by one device's query blocks.
All inputs are finite; a program needn't handle non-finite values.
Results may differ from the reference program's by a relative error of at most 0.01.
Values may be sent and summed in bfloat16 or wider, within the bound.
No kernel may reach another device: no remote copies, remote signals or barrier semaphores. Data moves between devices by JAX's collectives and lax.ppermute only.
A program may use at most 64 MiB of HBM per device.

```python
import math
import jax
import jax.numpy as jnp
from jax import lax

HD = 128
KVH = 8
GROUP = 8
BLK = 512
TOPK = 8
QB = 8
CAP = 2
QBD = 16
FEAT = 8192
NBLK = 64
CTX = 32768
QBLOCKS = 1024
QROWS = 8192


def draw_queries(key, part):
    key = jax.random.fold_in(key, 7)
    base = jnp.clip(jax.random.normal(key, (QROWS, FEAT), jnp.float32), -6.0, 6.0)
    return base.astype(jnp.bfloat16)


def draw_key_cache(key, part):
    key = jax.random.fold_in(key, 11)
    base = jnp.clip(jax.random.normal(key, (CTX, KVH * HD), jnp.float32), -6.0, 6.0)
    return base.astype(jnp.bfloat16)


def draw_value_cache(key, part):
    key = jax.random.fold_in(key, 13)
    base = jnp.clip(jax.random.normal(key, (CTX, KVH, HD), jnp.float32), -6.0, 6.0)
    rising = 3.0 ** (jnp.arange(KVH, dtype=jnp.float32) / (KVH - 1))
    return (base * rising[None, :, None]).reshape(CTX, KVH * HD).astype(jnp.bfloat16)


def draw_selected(key, part):
    key = jax.random.fold_in(key, 5)
    device = jnp.arange(NBLK)[:, None]
    blocks = jnp.arange(NBLK)[None, :]
    noise = jax.random.randint(key, (NBLK, NBLK), 0, 1000)
    score = noise + 600 * (blocks >= device - 8).astype(jnp.int32) + 400 * (blocks == 0).astype(jnp.int32)
    distinct = jnp.where(blocks < device, score * NBLK + blocks, -1 - blocks)
    ranking = jnp.argsort(-distinct, axis=1)
    group_ids = jnp.arange(QBLOCKS)
    owner = group_ids // QBD
    member = group_ids % QBD
    taken = jnp.minimum(TOPK - 1, CAP * owner // QBD)
    span = jnp.maximum(QBD * taken // CAP, 1)
    column = jnp.arange(TOPK - 1)[None, :]
    spot = (member[:, None] * taken[:, None] + column) % span[:, None]
    picked = ranking[owner[:, None], spot]
    picked = jnp.where(column < taken[:, None], picked, -1)
    return jnp.concatenate([owner[:, None], picked], axis=1).astype(jnp.int32)


def touch_ends(array, key, least, largest):
    extent = array.shape
    spot = [jax.random.randint(jax.random.fold_in(key, axis), (), 0, extent[axis]) for axis in range(len(extent))]
    array = array.at[tuple(spot)].set(least)
    longest = extent.index(max(extent))
    spot[longest] = (spot[longest] + 1) % extent[longest]
    return array.at[tuple(spot)].set(largest)


def setup_inputs(seed: int = 0) -> dict:
    seeds = jax.random.split(jax.random.key(seed), 7)
    return {
        "queries": draw_queries(jax.random.fold_in(seeds[6], 71), 0),
        "key_cache": draw_key_cache(jax.random.fold_in(seeds[6], 71), 0),
        "value_cache": draw_value_cache(jax.random.fold_in(seeds[6], 71), 0),
        "offsets": touch_ends(jax.random.randint(seeds[3], (QBLOCKS,), 0, BLK - QB + 1), jax.random.fold_in(seeds[3], 1), 0, BLK - QB).astype(jnp.int32),
        "selected": draw_selected(jax.random.fold_in(seeds[6], 71), 0),
        "out_gain": jnp.clip(1.0 + 0.1 * jax.random.normal(seeds[5], (FEAT,), jnp.float32), 0.5, 1.5).astype(jnp.bfloat16),
    }


def attend(query_rows, key_block, value_block, visible):
    scaling = 1.0 / math.sqrt(HD)
    scores = jnp.einsum('rkgd,jkd->rkgj', query_rows.astype(jnp.float32), key_block.astype(jnp.float32)) * scaling
    scores = jnp.where(visible, scores, -jnp.inf)
    row_peak = lax.optimization_barrier(jnp.max(scores, axis=-1))
    weights = jnp.exp(scores - row_peak[..., None])
    row_total = lax.optimization_barrier(jnp.sum(weights, axis=-1))
    probability = weights.astype(jnp.bfloat16)
    mixed_out = jnp.einsum('rkgj,jkd->rkgd', probability.astype(jnp.float32), value_block.astype(jnp.float32))
    mixed_out = mixed_out / row_total[..., None]
    return (mixed_out.astype(jnp.bfloat16), row_peak, row_total)

def reference(queries, key_cache, value_cache, offsets, selected, out_gain):
    key_blocks = key_cache.reshape(NBLK, BLK, KVH, HD)
    value_blocks = value_cache.reshape(NBLK, BLK, KVH, HD)
    within = jnp.arange(BLK, dtype=jnp.int32)
    everywhere = jnp.ones((1, 1, 1, BLK), dtype=bool)

    def one_block(group_index):
        first_row = (group_index * QB).astype(jnp.int32)
        query_rows = lax.dynamic_slice_in_dim(queries, first_row, QB, 0).reshape(QB, KVH, GROUP, HD)
        chosen = selected[group_index]
        last_key = offsets[group_index] + jnp.arange(QB, dtype=jnp.int32)
        causal = (within[None, :] <= last_key[:, None])[:, None, None, :]
        partials, peak_list, total_list, valid_list = ([], [], [], [])
        for entry in range(TOPK):
            block_id = chosen[entry]
            is_valid = block_id >= 0
            safe_block = jnp.maximum(block_id, 0)
            visible = causal if entry == 0 else everywhere
            mixed_out, row_peak, row_total = attend(query_rows, key_blocks[safe_block], value_blocks[safe_block], visible)
            partials.append(mixed_out.astype(jnp.float32))
            peak_list.append(jnp.where(is_valid, row_peak, -jnp.inf))
            total_list.append(row_total)
            valid_list.append(is_valid)
        peak_all = lax.optimization_barrier(jnp.max(jnp.stack(peak_list), axis=0))
        numerator = jnp.zeros((QB, KVH, GROUP, HD), jnp.float32)
        denominator = jnp.zeros((QB, KVH, GROUP), jnp.float32)
        for entry in range(TOPK):
            weight = jnp.where(valid_list[entry], total_list[entry] * jnp.exp(peak_list[entry] - peak_all), 0.0)
            numerator = numerator + weight[..., None] * partials[entry]
            denominator = denominator + weight
        return (numerator / denominator[..., None]).reshape(QB, FEAT)
    attended = lax.map(one_block, jnp.arange(QBLOCKS, dtype=jnp.int32)).reshape(QROWS, FEAT)
    mean_square = lax.optimization_barrier(jnp.sum(attended * attended, axis=-1, keepdims=True)) / FEAT
    normed = attended * lax.rsqrt(mean_square + 1e-06) * out_gain.astype(jnp.float32)[None, :]
    return normed.astype(jnp.bfloat16)
```

```python
import math

import jax
import jax.numpy as jnp
from jax import lax
from jax.experimental import pallas as pl
from jax.experimental.pallas import tpu as pltpu
from jax.sharding import Mesh
from jax.sharding import PartitionSpec as P

HD = 128
HEADS = 8
BLK = 512
CAP = 2
FEAT = 8192
ROWS_Y = 8
COLS_X = 4
QBLK = 16
QB = 8
QR = QB * HEADS
MSG = QBLK + 1
DUMMY = QBLK
LOW = -1e30
SCALE = math.log2(math.e) / math.sqrt(HD)

f32 = jnp.float32
bf16 = jnp.bfloat16
VMEM = pl.BlockSpec(memory_space=pltpu.VMEM)
SMEM = pl.BlockSpec(memory_space=pltpu.SMEM)


def call(kernel, outs, operands, specs, scratch=(), mib=16, flops=0, size=0):
    return pl.pallas_call(
        kernel,
        out_shape=outs,
        in_specs=specs,
        out_specs=jax.tree.map(lambda _: VMEM, outs),
        scratch_shapes=list(scratch),
        compiler_params=pltpu.CompilerParams(vmem_limit_bytes=mib * 2**20),
        cost_estimate=pl.CostEstimate(flops=flops, bytes_accessed=size, transcendentals=0),
    )(*operands)


def join_kernel(k_ref, v_ref, kv_ref):
    kv_ref[:BLK, :] = k_ref[...]
    kv_ref[BLK:, :] = v_ref[...]


def pack_kernel(q_ref, sel_ref, out_ref):
    for pair in range(QBLK // 2):
        rows = q_ref[pair * 16 : pair * 16 + 16, :].astype(f32)
        for half in range(2):
            part = rows[half * QB : half * QB + QB]
            tile = jnp.concatenate([part[:, h * HD : (h + 1) * HD] for h in range(HEADS)], axis=0).astype(bf16)
            for s in range(COLS_X):
                out_ref[s, pair * 2 + half] = tile
    sel = jnp.concatenate([sel_ref[...].astype(f32), jnp.zeros((QBLK, HD - 8), f32)], axis=1)
    tile = jnp.concatenate([sel, jnp.zeros((QR - QBLK, HD), f32)], axis=0).astype(bf16)
    for s in range(COLS_X):
        out_ref[s, QBLK] = tile


def scores_of(q, k):
    return lax.dot_general(q, k, (((1,), (1,)), ((), ())), preferred_element_type=f32) * SCALE


def with_ones(v):
    return jnp.concatenate([v, jnp.ones((BLK, HD), bf16)], axis=1)


def own_kernel(off_ref, q_ref, kv_ref, out_ref, lse_ref):
    k = kv_ref[:BLK, :]
    v = with_ones(kv_ref[BLK:, :])
    ahead = lax.broadcasted_iota(jnp.int32, (QR, BLK), 1) - lax.rem(
        lax.broadcasted_iota(jnp.int32, (QR, BLK), 0), QB
    )
    lane = lax.rem(lax.broadcasted_iota(jnp.int32, (QR, HD), 1), QBLK)
    lse = jnp.full((QR, HD), LOW, f32)
    for first in range(0, QBLK, 4):
        q = jnp.concatenate([q_ref[0, first + i] for i in range(4)], axis=0)
        s = scores_of(q, k)
        s = jnp.concatenate(
            [jnp.where(ahead <= off_ref[first + i], s[i * QR : (i + 1) * QR], LOW) for i in range(4)], axis=0
        )
        peak = jnp.max(s, axis=1, keepdims=True)
        p = jnp.exp2(s - peak).astype(bf16)
        o = jnp.dot(p, v, preferred_element_type=f32)
        total = o[:, HD:]
        mixed = o[:, :HD] / total
        entry = peak + jnp.log2(total)
        for i in range(4):
            out_ref[first + i] = mixed[i * QR : (i + 1) * QR]
            lse = jnp.where(lane == first + i, entry[i * QR : (i + 1) * QR], lse)
    lse_ref[...] = lse


def serve_kernel(index_ref, q_ref, *refs):
    blocks, (out_ref, acc, peak, total, qbuf) = refs[:-5], refs[-5:]
    acc[...] = jnp.zeros_like(acc)
    total[...] = jnp.zeros_like(total)
    peak[...] = jnp.full_like(peak, LOW)
    per = COLS_X * CAP
    j = 0
    for ref in blocks:
        for start in range(0, ref.shape[0], 2 * BLK):
            k = ref[start : start + BLK, :]
            v = with_ones(ref[start + BLK : start + 2 * BLK, :])
            for first in range(0, per, 4):
                ids = [index_ref[j * per + first + i] for i in range(4)]
                q = jnp.concatenate([q_ref[t] for t in ids], axis=0)
                s = scores_of(q, k)
                before = jnp.concatenate([peak[t] for t in ids], axis=0)
                now = jnp.maximum(before, jnp.max(s, axis=1, keepdims=True))
                p = jnp.exp2(s - jnp.concatenate([now] * (BLK // HD), axis=1)).astype(bf16)
                o = jnp.dot(p, v, preferred_element_type=f32)
                keep = jnp.exp2(before - now)
                for i, t in enumerate(ids):
                    part = slice(i * QR, (i + 1) * QR)
                    acc[t] = acc[t] * keep[part] + o[part, :HD]
                    total[t] = total[t] * keep[part] + o[part, HD:]
                    peak[t] = now[part]
            j += 1
    lanes = lax.broadcasted_iota(jnp.int32, (QR, HD), 1)
    lane = lax.rem(lanes, QBLK)
    for s in range(COLS_X):
        lse = jnp.full((QR, HD), LOW, f32)
        for g in range(QBLK):
            t = s * MSG + g
            tot = total[t]
            used = tot > 0.0
            safe = jnp.where(used, tot, 1.0)
            out_ref[s, g] = (acc[t] / safe).astype(bf16)
            lse = jnp.where(lane == g, jnp.where(used, peak[t] + jnp.log2(safe), LOW), lse)
        high = lse.astype(bf16).astype(f32)
        middle = (lse - high).astype(bf16).astype(f32)
        low = lse - high - middle
        out_ref[s, QBLK] = jnp.where(lanes < QBLK, high, jnp.where(lanes < 2 * QBLK, middle, low)).astype(bf16)


def combine_kernel(back_ref, own_ref, own_lse_ref, att_ref, squares_ref):
    lses = []
    for s in range(COLS_X):
        st = back_ref[s, QBLK].astype(f32)
        lses.append(st + pltpu.roll(st, HD - QBLK, 1) + pltpu.roll(st, HD - 2 * QBLK, 1))
    lses.append(own_lse_ref[...])
    most = lses[0]
    for e in lses[1:]:
        most = jnp.maximum(most, e)
    weights = [jnp.exp2(e - most) for e in lses]
    inverse = 1.0 / sum(weights)
    weights = [w * inverse for w in weights]
    lane = lax.broadcasted_iota(jnp.int32, (QB, HD), 1)
    squares = jnp.zeros((QB, HD), f32)
    for g in range(QBLK):
        a = weights[COLS_X][:, g : g + 1] * own_ref[g]
        for s in range(COLS_X):
            a = a + weights[s][:, g : g + 1] * back_ref[s, g].astype(f32)
        att_ref[g] = a
        sq = a * a
        rows = sq[:QB]
        for h in range(1, HEADS):
            rows = rows + sq[h * QB : (h + 1) * QB]
        squares = jnp.where(lane == g, jnp.sum(rows, axis=1, keepdims=True), squares)
    for z in range(squares_ref.shape[0]):
        squares_ref[z] = squares


def norm_kernel(att_ref, squares_ref, gain_ref, out_ref):
    squares = squares_ref[0]
    for z in range(1, squares_ref.shape[0]):
        squares = squares + squares_ref[z]
    scale = lax.rsqrt(squares * (1.0 / FEAT) + 1e-06)
    for pair in range(QBLK // 2):
        halves = []
        for g in (2 * pair, 2 * pair + 1):
            factor = jnp.broadcast_to(scale[:, g : g + 1], (QB, HD))
            halves.append(
                jnp.concatenate([att_ref[g, h * QB : (h + 1) * QB, :] * factor for h in range(HEADS)], axis=1)
            )
        rows = jnp.concatenate(halves, axis=0) * gain_ref[...].astype(f32)
        out_ref[pair * 16 : pair * 16 + 16, :] = rows.astype(bf16)


def index_of(selected, blocks):
    hit = jnp.any(selected[:, :, :, None] == blocks[None, None, None, :], axis=2)
    count = hit.astype(jnp.int32)
    earlier = jnp.tril(jnp.ones((QBLK, QBLK), jnp.int32), -1)
    rank = jnp.sum(earlier[None, :, :, None] * count[:, None, :, :], axis=2)
    name = jnp.arange(COLS_X, dtype=jnp.int32)[:, None] * MSG + jnp.arange(QBLK, dtype=jnp.int32)[None, :]
    slots = []
    for c in range(CAP):
        here = hit & (rank == c)
        slots.append(DUMMY + jnp.sum(jnp.where(here, name[:, :, None] - DUMMY, 0), axis=1))
    return jnp.stack(slots, axis=-1).transpose(1, 0, 2).reshape(-1)


def body(queries, key_cache, value_cache, offsets, selected, out_gain):
    y, x, core = lax.axis_index("y"), lax.axis_index("x"), lax.axis_index("core")
    sds = jax.ShapeDtypeStruct
    kv = call(join_kernel, sds((2 * BLK, HD), bf16), (key_cache, value_cache), [VMEM] * 2, size=2**19)

    def up(a, k):
        return lax.ppermute(a, "y", [(i, i + 1) for i in range(k - 1, ROWS_Y - 1)])

    def down(a, k):
        return lax.ppermute(a, "y", [((i - k + 1) % ROWS_Y, (i - k) % ROWS_Y) for i in range(3)])

    def swap(a):
        return lax.ppermute(a, "core", [(0, 1), (1, 0)])

    up1, down1 = up(kv, 1), down(kv, 1)
    packed = call(pack_kernel, sds((COLS_X, MSG, QR, HD), bf16), (queries, selected), [VMEM] * 2, size=2**21)
    asked = lax.all_to_all(packed, "x", split_axis=0, concat_axis=0, tiled=True)
    far = lax.ppermute(kv, "y", [(i, i + 4) for i in range(4)])
    up2, down2 = up(up1, 2), down(down1, 2)
    up3, down3 = up(up2, 3), down(down2, 3)
    group1 = jnp.concatenate([up1, down1], axis=0)
    group2 = jnp.concatenate([up2, down2, far], axis=0)
    group3 = jnp.concatenate([up3, down3], axis=0)
    held = [kv, swap(kv), group1, swap(group1), group2, swap(group2), group3, swap(group3)]
    column = []
    for shifts in ((0,), (1, 7), (2, 6, 4), (3, 5)):
        for c in (core, 1 - core):
            column += [lax.rem(y + ROWS_Y - k, ROWS_Y) * (2 * COLS_X) + x * 2 + c for k in shifts]
    own, own_lse = call(
        own_kernel,
        (sds((QBLK, QR, HD), f32), sds((QR, HD), f32)),
        (offsets, packed, kv),
        [SMEM, VMEM, VMEM],
        flops=2**28,
        size=2**21,
    )
    wanted = asked[:, QBLK, :QBLK, 1:8].astype(jnp.int32)
    index = index_of(wanted, jnp.stack(column).astype(jnp.int32))
    slots = COLS_X * MSG
    served = call(
        serve_kernel,
        sds((COLS_X, MSG, QR, HD), bf16),
        (index, asked.reshape(slots, QR, HD), *held),
        [SMEM] + [VMEM] * (1 + len(held)),
        scratch=[pltpu.VMEM((slots, QR, HD), f32)] * 3 + [pltpu.VMEM((BLK, HD), bf16)],
        mib=40,
        flops=2**31,
        size=2**23,
    )
    back = lax.all_to_all(served, "x", split_axis=0, concat_axis=0, tiled=True)
    att, squares = call(
        combine_kernel,
        (sds((QBLK, QR, HD), f32), sds((8, QB, HD), f32)),
        (back, own, own_lse),
        [VMEM] * 3,
        size=2**21,
    )
    squares = lax.all_to_all(squares, "head", split_axis=0, concat_axis=0, tiled=True)
    return call(
        norm_kernel,
        sds((QBLK * QB, HEADS * HD), bf16),
        (att, squares, out_gain.reshape(1, HEADS * HD)),
        [VMEM] * 3,
        size=2**20,
    )


def solution(mesh):
    grid = Mesh(mesh.devices.reshape(ROWS_Y, COLS_X, 2, mesh.shape["head"]), ("y", "x", "core", "head"))
    ctx = ("y", "x", "core")
    placed = (P(ctx, "head"), P(ctx, "head"), P(ctx, "head"), P(ctx), P(ctx, None), P("head"))
    return jax.shard_map(body, mesh=grid, in_specs=placed, out_specs=P(ctx, "head"), check_vma=False)
```

```python
import math

import jax
import jax.numpy as jnp
from jax import lax
from jax.experimental import pallas as pl
from jax.experimental.pallas import tpu as pltpu
from jax.sharding import Mesh
from jax.sharding import PartitionSpec as P

HD = 128
HEADS = 8
BLK = 512
CAP = 2
FEAT = 8192
ROWS_Y = 8
COLS_X = 4
QBLK = 16
QB = 8
QR = QB * HEADS
MSG = QBLK + 1
DUMMY = QBLK
LOW = -1e30
SCALE = math.log2(math.e) / math.sqrt(HD)

f32 = jnp.float32
bf16 = jnp.bfloat16
VMEM = pl.BlockSpec(memory_space=pltpu.VMEM)
SMEM = pl.BlockSpec(memory_space=pltpu.SMEM)


def call(kernel, outs, operands, specs, mib=16, flops=0, size=0, aliases=None, scratch=()):
    return pl.pallas_call(
        kernel,
        out_shape=outs,
        in_specs=specs,
        out_specs=jax.tree.map(lambda _: VMEM, outs),
        scratch_shapes=list(scratch),
        input_output_aliases=aliases or {},
        compiler_params=pltpu.CompilerParams(vmem_limit_bytes=mib * 2**20),
        cost_estimate=pl.CostEstimate(flops=flops, bytes_accessed=size, transcendentals=0),
    )(*operands)


def join_kernel(*refs):
    *parts, out_ref, sems = refs
    copies = []
    row = 0
    for i, ref in enumerate(parts):
        copies.append(pltpu.make_async_copy(ref, out_ref.at[row : row + ref.shape[0], :], sems.at[i]))
        row += ref.shape[0]
    for copy in copies:
        copy.start()
    for copy in copies:
        copy.wait()


def join(parts):
    return call(
        join_kernel,
        jax.ShapeDtypeStruct((sum(p.shape[0] for p in parts), HD), bf16),
        parts,
        [pl.BlockSpec(memory_space=pl.ANY)] * len(parts),
        mib=63,
        size=2**20,
        scratch=[pltpu.SemaphoreType.DMA((len(parts),))],
    )


def pack_kernel(q_ref, sel_ref, out_ref):
    for pair in range(QBLK // 2):
        rows = q_ref[pair * 16 : pair * 16 + 16, :].astype(f32)
        for half in range(2):
            part = rows[half * QB : half * QB + QB]
            tile = jnp.concatenate([part[:, h * HD : (h + 1) * HD] for h in range(HEADS)], axis=0).astype(bf16)
            for s in range(COLS_X):
                out_ref[s, pair * 2 + half] = tile
    sel = jnp.concatenate([sel_ref[...].astype(f32), jnp.zeros((QBLK, HD - 8), f32)], axis=1)
    tile = jnp.concatenate([sel, jnp.zeros((QR - QBLK, HD), f32)], axis=0).astype(bf16)
    for s in range(COLS_X):
        out_ref[s, QBLK] = tile


def scores_of(q, k):
    return lax.dot_general(q, k, (((1,), (1,)), ((), ())), preferred_element_type=f32) * SCALE


def with_ones(v):
    return jnp.concatenate([v, jnp.ones((BLK, HD), bf16)], axis=1)


def own_kernel(off_ref, q_ref, kv_ref, out_ref, peak_ref, total_ref):
    k = kv_ref[:BLK, :]
    v = with_ones(kv_ref[BLK:, :])
    ahead = lax.broadcasted_iota(jnp.int32, (QR, BLK), 1) - lax.rem(
        lax.broadcasted_iota(jnp.int32, (QR, BLK), 0), QB
    )
    lane = lax.broadcasted_iota(jnp.int32, (QR, HD), 1)
    peaks = jnp.zeros((QR, HD), f32)
    totals = jnp.ones((QR, HD), f32)
    for first in range(0, QBLK, 4):
        q = jnp.concatenate([q_ref[0, first + i] for i in range(4)], axis=0)
        s = scores_of(q, k)
        s = jnp.concatenate(
            [jnp.where(ahead <= off_ref[first + i], s[i * QR : (i + 1) * QR], LOW) for i in range(4)], axis=0
        )
        peak = jnp.max(s, axis=1, keepdims=True)
        p = jnp.exp2(s - peak).astype(bf16)
        o = jnp.dot(p, v, preferred_element_type=f32)
        for i in range(4):
            part = slice(i * QR, (i + 1) * QR)
            out_ref[first + i] = o[part, :HD]
            peaks = jnp.where(lane == first + i, peak[part], peaks)
            totals = jnp.where(lane == first + i, o[part, HD:], totals)
    peak_ref[...] = peaks
    total_ref[...] = totals


def merge(index_ref, first_block, q_ref, blocks, acc, peak, total):
    per = COLS_X * CAP
    j = first_block
    for ref in blocks:
        for start in range(0, ref.shape[0], 2 * BLK):
            k = ref[start : start + BLK, :]
            v = with_ones(ref[start + BLK : start + 2 * BLK, :])
            for first in range(0, per, 4):
                ids = [index_ref[j * per + first + i] for i in range(4)]
                q = jnp.concatenate([q_ref[t] for t in ids], axis=0)
                s = scores_of(q, k)
                before = jnp.concatenate([peak[t] for t in ids], axis=0)
                now = jnp.maximum(before, jnp.max(s, axis=1, keepdims=True))
                p = jnp.exp2(s - jnp.concatenate([now] * (BLK // HD), axis=1)).astype(bf16)
                o = jnp.dot(p, v, preferred_element_type=f32)
                keep = jnp.exp2(before - now)
                for i, t in enumerate(ids):
                    part = slice(i * QR, (i + 1) * QR)
                    acc[t] = acc[t] * keep[part] + o[part, :HD]
                    total[t] = total[t] * keep[part] + o[part, HD:]
                    peak[t] = now[part]
            j += 1


def serve_kernel(index_ref, q_ref, *refs):
    *blocks, out_ref, acc, peak, total = refs
    acc[...] = jnp.zeros_like(acc)
    total[...] = jnp.zeros_like(total)
    peak[...] = jnp.full_like(peak, LOW)
    merge(index_ref, 0, q_ref, blocks, acc, peak, total)
    lanes = lax.broadcasted_iota(jnp.int32, (QR, HD), 1)
    lane = lax.rem(lanes, QBLK)
    term = lax.rem(lax.div(lanes, QBLK), 3)
    for s in range(COLS_X):
        both = jnp.zeros((QR, HD), f32)
        for g in range(QBLK):
            t = s * MSG + g
            out_ref[s, g] = acc[t].astype(bf16)
            both = jnp.where(lane == g, jnp.where(lanes < 3 * QBLK, peak[t], total[t]), both)
        high = both.astype(bf16).astype(f32)
        middle = (both - high).astype(bf16).astype(f32)
        low = both - high - middle
        out_ref[s, QBLK] = jnp.where(term == 0, high, jnp.where(term == 1, middle, low)).astype(bf16)


def combine_kernel(back_ref, own_ref, own_peak_ref, own_total_ref, att_ref, squares_ref):
    peaks = [own_peak_ref[...]]
    totals = [own_total_ref[...]]
    for s in range(COLS_X):
        terms = back_ref[s, QBLK].astype(f32)
        both = terms + pltpu.roll(terms, HD - QBLK, 1) + pltpu.roll(terms, HD - 2 * QBLK, 1)
        peaks.append(both)
        totals.append(pltpu.roll(both, HD - 3 * QBLK, 1))
    most = peaks[0]
    for e in peaks[1:]:
        most = jnp.maximum(most, e)
    weights = [jnp.exp2(e - most) for e in peaks]
    inverse = 1.0 / sum(w * t for w, t in zip(weights, totals))
    weights = [w * inverse for w in weights]
    lane = lax.broadcasted_iota(jnp.int32, (QB, HD), 1)
    squares = jnp.zeros((QB, HD), f32)
    for g in range(QBLK):
        a = weights[0][:, g : g + 1] * own_ref[g]
        for s in range(COLS_X):
            a = a + weights[s + 1][:, g : g + 1] * back_ref[s, g].astype(f32)
        att_ref[g] = a
        sq = a * a
        rows = sq[:QB]
        for h in range(1, HEADS):
            rows = rows + sq[h * QB : (h + 1) * QB]
        squares = jnp.where(lane == g, jnp.sum(rows, axis=1, keepdims=True), squares)
    for z in range(squares_ref.shape[0]):
        squares_ref[z] = squares


def norm_kernel(att_ref, squares_ref, gain_ref, out_ref):
    squares = squares_ref[0]
    for z in range(1, squares_ref.shape[0]):
        squares = squares + squares_ref[z]
    scale = lax.rsqrt(squares * (1.0 / FEAT) + 1e-06)
    for pair in range(QBLK // 2):
        halves = []
        for g in (2 * pair, 2 * pair + 1):
            factor = jnp.broadcast_to(scale[:, g : g + 1], (QB, HD))
            halves.append(
                jnp.concatenate([att_ref[g, h * QB : (h + 1) * QB, :] * factor for h in range(HEADS)], axis=1)
            )
        rows = jnp.concatenate(halves, axis=0) * gain_ref[...].astype(f32)
        out_ref[pair * 16 : pair * 16 + 16, :] = rows.astype(bf16)


def index_of(selected, blocks):
    hit = jnp.any(selected[:, :, :, None] == blocks[None, None, None, :], axis=2)
    count = hit.astype(jnp.int32)
    earlier = jnp.tril(jnp.ones((QBLK, QBLK), jnp.int32), -1)
    rank = jnp.sum(earlier[None, :, :, None] * count[:, None, :, :], axis=2)
    name = jnp.arange(COLS_X, dtype=jnp.int32)[:, None] * MSG + jnp.arange(QBLK, dtype=jnp.int32)[None, :]
    slots = []
    for c in range(CAP):
        here = hit & (rank == c)
        slots.append(DUMMY + jnp.sum(jnp.where(here, name[:, :, None] - DUMMY, 0), axis=1))
    return jnp.stack(slots, axis=-1).transpose(1, 0, 2).reshape(-1)


def body(queries, key_cache, value_cache, offsets, selected, out_gain):
    y, x, core = lax.axis_index("y"), lax.axis_index("x"), lax.axis_index("core")
    sds = jax.ShapeDtypeStruct
    kv = join((key_cache, value_cache))

    def up(a, k):
        return lax.ppermute(a, "y", [(i, i + 1) for i in range(k - 1, ROWS_Y - 1)])

    def down(a, k):
        return lax.ppermute(a, "y", [((i - k + 1) % ROWS_Y, (i - k) % ROWS_Y) for i in range(3)])

    def swap(a):
        return lax.ppermute(a, "core", [(0, 1), (1, 0)])

    up1, down1 = up(kv, 1), down(kv, 1)
    packed = call(pack_kernel, sds((COLS_X, MSG, QR, HD), bf16), (queries, selected), [VMEM] * 2, size=2**21)
    asked = lax.all_to_all(packed, "x", split_axis=0, concat_axis=0, tiled=True)
    far = lax.ppermute(kv, "y", [(2, 6), (3, 7)])
    down2 = lax.ppermute(kv, "y", [(0, 6), (1, 7), (2, 0)])
    up2 = up(up1, 2)
    round_back = lax.ppermute(down2, "y", [(6, 4), (7, 5)])
    down3 = down(down2, 3)
    far, up2 = lax.optimization_barrier((far, up2))
    up3 = up(up2, 3)
    held = [kv, swap(kv)]
    for group in ((up1, down1, down2), (up2, down3), (up3, jnp.where(y < 6, round_back, far))):
        group = jnp.concatenate(group, axis=0) if len(group) > 1 else group[0]
        held += [group, swap(group)]
    column = []
    for shifts in ((0,), (1, 7, 6), (2, 5), (3, 4)):
        for c in (core, 1 - core):
            column += [lax.rem(y + ROWS_Y - k, ROWS_Y) * (2 * COLS_X) + x * 2 + c for k in shifts]
    own = call(
        own_kernel,
        (sds((QBLK, QR, HD), f32), sds((QR, HD), f32), sds((QR, HD), f32)),
        (offsets, packed, kv),
        [SMEM, VMEM, VMEM],
        flops=2**28,
        size=2**21,
    )
    wanted = asked[:, QBLK, :QBLK, 1:8].astype(jnp.int32)
    index = index_of(wanted, jnp.stack(column).astype(jnp.int32))
    slots = COLS_X * MSG
    asked = asked.reshape(slots, QR, HD)
    served = call(
        serve_kernel,
        sds((COLS_X, MSG, QR, HD), bf16),
        (index, asked, *held),
        [SMEM] + [VMEM] * (1 + len(held)),
        mib=32,
        flops=16 * 2**27,
        size=2**23,
        scratch=[pltpu.VMEM((slots, QR, HD), f32)] * 3,
    )
    back = lax.all_to_all(served, "x", split_axis=0, concat_axis=0, tiled=True)
    att, squares = call(
        combine_kernel,
        (sds((QBLK, QR, HD), f32), sds((8, QB, HD), f32)),
        (back, *own),
        [VMEM] * 4,
        size=2**21,
    )
    squares = lax.all_to_all(squares, "head", split_axis=0, concat_axis=0, tiled=True)
    return call(
        norm_kernel,
        sds((QBLK * QB, HEADS * HD), bf16),
        (att, squares, out_gain.reshape(1, HEADS * HD)),
        [VMEM] * 3,
        size=2**20,
    )


def solution(mesh):
    grid = Mesh(mesh.devices.reshape(ROWS_Y, COLS_X, 2, mesh.shape["head"]), ("y", "x", "core", "head"))
    ctx = ("y", "x", "core")
    placed = (P(ctx, "head"), P(ctx, "head"), P(ctx, "head"), P(ctx), P(ctx, None), P("head"))
    return jax.shard_map(body, mesh=grid, in_specs=placed, out_specs=P(ctx, "head"), check_vma=False)
```
